128 devices in a mesh: dp: 8 (over x, y_hi), seq: 16 (over z, y_lo, core).
Axes of the slice: x: 4, y: 4 (y_hi: 2, y_lo: 2; y = y_hi * 2 + y_lo), z: 4, core: 2. Of those that a mesh axis runs over, the one named last changes fastest.
Arguments:
- tokens: bfloat16 [8, 16, 384, 3072], P('dp', 'seq'), may hold values from -45 to 45
- spatial_query: bfloat16 [8, 16, 384, 1536], P('dp', 'seq'), may hold values from -100 to 100
- spatial_key: bfloat16 [8, 16, 384, 1536], P('dp', 'seq'), may hold values from -6 to 6
- spatial_value: bfloat16 [8, 16, 384, 1536], P('dp', 'seq'), may hold values from -6 to 6
- out_weight: bfloat16 [1536, 3072], P('dp', 'seq'), may hold values from -0.15625 to 0.15625
- qkv_weight: bfloat16 [3072, 4608], P('dp', 'seq'), may hold values from -0.09021098 to 0.09021098
- modulation: float32 [8, 3, 3072], P('dp'), may hold values from -4 to 4
- query_gain: float32 [128], replicated, may hold values from 0.5 to 6
- key_gain: float32 [128], replicated, may hold values from 0.5 to 6
Outputs:
- temporal_out: bfloat16 [8, 16, 384, 1536], P('dp', None, 'seq')
The draws below stay inside these ranges and needn't reach their ends.
All inputs are finite; a program needn't handle non-finite values.
Results may differ from the reference program's by a relative error of at most 0.025.
Values may be sent and summed in bfloat16 or wider, within the bound.
A program may use at most 128 MiB of HBM per device.

```python
import math
import jax
import jax.numpy as jnp
from jax import lax

D = 3072
HD = 128
HEADS = 12
S = 384
HW = 1536
F = 16
B = 8


def spread_scales(key, shape, low, high):
    return jnp.exp(jax.random.uniform(key, shape, jnp.float32, math.log(low), math.log(high)))


def draw_tokens(key, part):
    key = jax.random.fold_in(key, 11)
    first, second, third = jax.random.split(key, 3)
    rows = spread_scales(first, (B, F, S, 1), 0.3, 3.0)
    cols = spread_scales(second, (D,), 0.3, 3.0)
    base = jnp.clip(jax.random.normal(third, (B, F, S, D), jnp.float32), -5.0, 5.0)
    return (base * rows * cols).astype(jnp.bfloat16)


def drawn_parts(key):
    first = jax.random.fold_in(key, 0)
    base = jnp.clip(jax.random.normal(first, (B, F, S, HEADS * HD), jnp.float32), -5.0, 5.0)
    return base


def draw_spatial_key(key, part):
    base = drawn_parts(key)
    return base.astype(jnp.bfloat16)


def draw_spatial_query(key, part):
    key = jax.random.fold_in(key, 22)
    own = jnp.clip(jax.random.normal(key, (B, F, S, HEADS * HD), jnp.float32), -5.0, 5.0)
    return (2.0 * own).astype(jnp.bfloat16)


def draw_qkv_weight(key, part):
    key = jax.random.fold_in(key, 31)
    width = HEADS * HD
    full = jnp.clip(jax.random.normal(key, (D, 3 * width), jnp.float32), -4.95, 4.95) * D ** (-0.5)
    return full.astype(jnp.bfloat16)


def draw_query_gain(key, part):
    key = jax.random.fold_in(key, 41)
    return spread_scales(key, (HD,), 0.5, 2.0)


def draw_key_gain(key, part):
    key = jax.random.fold_in(key, 42)
    return spread_scales(key, (HD,), 0.5, 2.0)


def steps_of(key, shape, cuts, smallest, high):
    level = 1.0
    for position, parts in cuts:
        draws = jax.random.uniform(jax.random.fold_in(jax.random.fold_in(key, 6), position), (parts,), jnp.float32, smallest / len(cuts), high / len(cuts))
        level = level * jnp.repeat(jnp.exp(draws), shape[position] // parts).reshape((-1,) + (1,) * (len(shape) - 1 - position))
    return level


def bell_draw(stream_key, dims, deviation, reach, shards=(), kind=jnp.bfloat16):
    result = jax.random.normal(stream_key, dims, jnp.float32) * deviation
    if len(shards) > 0:
        result = steps_of(stream_key, dims, shards, -0.22, 0.18) * result
    return jnp.clip(result, min=-reach, max=reach).astype(kind)


def setup_inputs(seed: int = 0) -> dict:
    arg_keys = jax.random.split(jax.random.key(seed), 10)
    return {
        "tokens": draw_tokens(jax.random.fold_in(arg_keys[9], 71), 0),
        "spatial_query": draw_spatial_query(jax.random.fold_in(arg_keys[9], 71), 0),
        "spatial_key": draw_spatial_key(jax.random.fold_in(arg_keys[9], 71), 0),
        "spatial_value": bell_draw(arg_keys[3], (B, F, S, HW), 1.0, 6.0, ((0, 8), (1, 16))),
        "out_weight": bell_draw(arg_keys[4], (HW, D), HW ** -0.5, 0.15625, ((0, 8), (1, 16))),
        "qkv_weight": draw_qkv_weight(jax.random.fold_in(arg_keys[9], 71), 0),
        "modulation": bell_draw(arg_keys[6], (B, 3, D), 1.0, 4.0, ((0, 8),), jnp.float32),
        "query_gain": draw_query_gain(jax.random.fold_in(arg_keys[9], 71), 0),
        "key_gain": draw_key_gain(jax.random.fold_in(arg_keys[9], 71), 0),
    }


def spatial_frame(query, key, value):
    rows = query.shape[0]
    q = query.reshape(rows, HEADS, HD).astype(jnp.float32)
    k = key.reshape(rows, HEADS, HD).astype(jnp.float32)
    v = value.reshape(rows, HEADS, HD).astype(jnp.float32)
    scores = jnp.einsum('ihd,jhd->hij', q, k) / jnp.sqrt(jnp.float32(HD))
    probs = jax.nn.softmax(scores, axis=-1).astype(jnp.bfloat16)
    attn = jnp.einsum('hij,jhd->ihd', probs.astype(jnp.float32), v)
    return attn.astype(jnp.bfloat16).reshape(rows, HEADS * HD)

def head_norm(values, gain):
    wide = values.astype(jnp.float32)
    scale = lax.rsqrt(lax.optimization_barrier(jnp.mean(wide * wide, axis=-1, keepdims=True)) + 1e-06)
    return (wide * scale * gain).astype(jnp.bfloat16)

def temporal(qkv, query_gain, key_gain):
    query = head_norm(qkv[:, :, 0], query_gain).astype(jnp.float32)
    key = head_norm(qkv[:, :, 1], key_gain).astype(jnp.float32)
    value = qkv[:, :, 2].astype(jnp.float32)
    scores = jnp.einsum('fphd,gphd->phfg', query, key) / jnp.sqrt(jnp.float32(HD))
    probs = jax.nn.softmax(scores, axis=-1).astype(jnp.bfloat16)
    return jnp.einsum('phfg,gphd->fphd', probs.astype(jnp.float32), value).astype(jnp.bfloat16)

def reference(tokens, spatial_query, spatial_key, spatial_value, out_weight, qkv_weight, modulation, query_gain, key_gain):

    def one_sample(items):
        sample, query, key, value, mods = items
        frames, rows, width = sample.shape
        attn = lax.map(lambda trio: spatial_frame(trio[0], trio[1], trio[2]), (query, key, value))
        proj = jnp.dot(attn.reshape(frames * rows, HEADS * HD), out_weight, preferred_element_type=jnp.float32)
        mixed = (sample.reshape(frames * rows, width).astype(jnp.float32) + mods[0] * proj).astype(jnp.bfloat16)
        wide = mixed.astype(jnp.float32)
        mean = lax.optimization_barrier(jnp.mean(wide, axis=-1, keepdims=True))
        var = lax.optimization_barrier(jnp.mean((wide - mean) ** 2, axis=-1, keepdims=True))
        normed = ((wide - mean) * lax.rsqrt(var + 1e-06) * (1.0 + mods[2]) + mods[1]).astype(jnp.bfloat16)
        qkv = jnp.dot(normed, qkv_weight, preferred_element_type=jnp.float32).astype(jnp.bfloat16)
        qkv = qkv.reshape(frames, rows, 3, HEADS, HD)
        return temporal(qkv, query_gain, key_gain).reshape(frames, rows, HEADS * HD)
    return lax.map(one_sample, (tokens, spatial_query, spatial_key, spatial_value, modulation))
```

```python
import functools

import jax
import jax.numpy as jnp
from jax import lax
from jax.experimental import pallas as pl
from jax.experimental.pallas import tpu as pltpu
from jax.sharding import PartitionSpec as P

MESH = pl.DeviceIdType.MESH
BF = jnp.bfloat16
F32 = jnp.float32

W_PIECES = (("yzx", 0, 112, 64), ("zxy", 112, 96, 48), ("xyz", 208, 80, 48))
O_PIECES = (("yzx", 0, 32, 16), ("zxy", 32, 32, 16), ("xyz", 64, 32, 16))


def dot(a, b):
    return jnp.dot(a, b, preferred_element_type=F32)


def kernel(
    q_hbm, k_hbm, v_hbm, tok_hbm, ow, wt, mod, qg, kg, out_hbm,
    wbuf, obuf, acc, tok, qs, ks, vs, mix, moved, xt, ot, oin,
    load_sem, out_sem, ring_s, ring_r, near_s, near_r, oin_s, oin_r, a2a_s, a2a_r, fwd_s, fwd_r,
):
    dp = lax.axis_index("dp")
    seq = lax.axis_index("seq")
    x, z, c = dp // 2, seq // 4, seq % 2
    yl = (seq // 2) % 2
    y = (dp % 2) * 2 + yl
    me = {"x": x, "y": y, "z": z}
    chip = z * 2 + yl

    def device(at, core):
        return (at["x"] * 2 + at["y"] // 2, at["z"] * 4 + (at["y"] % 2) * 2 + core)

    def step(axis, by):
        return {**me, axis: lax.rem(me[axis] + by, 4)}

    def other_chip(t):
        return (dp, t * 2 + c)

    near = device(me, 1 - c)

    loads = [
        pltpu.make_async_copy(src, dst, load_sem.at[i])
        for i, (src, dst) in enumerate(((q_hbm, qs), (k_hbm, ks), (v_hbm, vs), (tok_hbm, tok)))
    ]
    for copy in loads:
        copy.start()

    wbuf[x, z, y, c] = wt[...]

    barrier = pltpu.get_barrier_semaphore()
    partners = [device(step(a, by), c) for a in "xyz" for by in (1, 3)] + [near]
    partners += [other_chip(lax.rem(chip + 2 * k, 8)) for k in (2,)]
    flip = z * 2 + (1 - yl)
    partners += [other_chip(lax.rem(flip + 2 * k, 8)) for k in (1, 2, 3)]
    for partner in partners:
        pl.semaphore_signal(barrier, inc=1, device_id=partner, device_id_type=MESH)
    pl.semaphore_wait(barrier, len(partners))

    pending = []

    def remote(src, dst, send, recv, to):
        return pltpu.make_async_remote_copy(
            src_ref=src, dst_ref=dst, send_sem=send, recv_sem=recv, device_id=to, device_id_type=MESH
        )

    def start(src, dst, send, recv, to):
        copy = remote(src, dst, send, recv, to)
        copy.start()
        pending.append(copy)

    def slot(buf, order, phase, shift, core, r0, n):
        index = {}
        for i, axis in enumerate(order):
            if i < phase:
                index[axis] = slice(None)
            elif i == phase:
                index[axis] = lax.rem(me[axis] + shift, 4)
            else:
                index[axis] = me[axis]
        return buf.at[index["x"], index["z"], index["y"], core, pl.ds(r0, n), :]

    class Piece:
        def __init__(self, buf, spec, base):
            self.buf = buf
            self.order, self.r0, self.n, self.half = spec
            self.base = base

        def part(self, phase, shift, which):
            r0, n = {
                "A": (self.r0, self.half),
                "B": (self.r0 + self.half, self.n - self.half),
                "W": (self.r0, self.n),
            }[which]
            return slot(self.buf, self.order, phase, shift, c, r0, n)

        def send(self, phase, way, k, shift, which):
            ref = self.part(phase, shift, which)
            i = self.base * 3 + phase
            to = device(step(self.order[phase], (1, 3)[way]), c)
            start(ref, ref, ring_s.at[i, way, k], ring_r.at[i, way, k], to)

        def wait(self, phase, way, k, shift, which):
            ref = self.part(phase, shift, which)
            i = self.base * 3 + phase
            remote(ref, ref, ring_s.at[i, way, k], ring_r.at[i, way, k], near).wait_recv()

        def own(self, phase):
            for way, names in ((0, "AB"), (1, "BA")):
                for k, which in enumerate(names):
                    self.send(phase, way, k, 0, which)

        def forward(self, phase):
            self.wait(phase, 0, 0, 3, "A")
            self.send(phase, 0, 2, 3, "A")
            self.wait(phase, 1, 0, 1, "B")
            self.send(phase, 1, 2, 1, "B")

        def rest(self, phase, sides=True, far=True):
            if sides:
                self.wait(phase, 0, 1, 3, "B")
                self.wait(phase, 1, 1, 1, "A")
            if far:
                self.wait(phase, 0, 2, 2, "A")
                self.wait(phase, 1, 2, 2, "B")

        def to_near(self, shift):
            ref = self.part(2, shift, "W")
            start(ref, ref, near_s.at[self.base, shift], near_r.at[self.base, shift], near)

        def from_near(self, shift):
            ref = slot(self.buf, self.order, 2, shift, 1 - c, self.r0, self.n)
            remote(ref, ref, near_s.at[self.base, shift], near_r.at[self.base, shift], near).wait_recv()

    ws = [Piece(wbuf, spec, i) for i, spec in enumerate(W_PIECES)]
    os = [Piece(obuf, spec, 3 + i) for i, spec in enumerate(O_PIECES)]

    half = ow.at[pl.ds(pl.multiple_of(96 * (1 - c), 16), 96), :]
    start(half, oin, oin_s, oin_r, near)
    for piece in ws:
        piece.own(0)
    row = lax.broadcasted_iota(jnp.int32, (192, 384), 0)
    col = lax.broadcasted_iota(jnp.int32, (192, 384), 1)
    mine = ow[pl.ds(pl.multiple_of(96 * c, 16), 96), :]
    block = dot(mine, (col - row == 192 * c).astype(F32).astype(BF))
    remote(oin, oin, oin_s, oin_r, near).wait_recv()
    block += dot(oin[...], (col - row == 192 * (1 - c)).astype(F32).astype(BF))
    obuf[x, z, y, c] = block.astype(BF)
    for piece in os:
        piece.own(0)

    for copy in loads[:3]:
        copy.wait()

    def heads(first, count):
        def body(h, _):
            cols = pl.ds(pl.multiple_of(h * 128, 128), 128)
            s = lax.dot_general(
                qs[:, cols], ks[:, cols], (((1,), (1,)), ((), ())), preferred_element_type=F32
            )
            s = s * (128**-0.5)
            e = jnp.exp(s - jnp.max(s, axis=1, keepdims=True))
            total = jnp.sum(e, axis=1, keepdims=True)
            o = dot(e.astype(BF), vs[:, cols])
            qs[:, cols] = (o / total).astype(BF)
            return 0

        lax.fori_loop(first, first + count, body, 0)

    heads(0, 2)
    for piece in os:
        piece.forward(0)
    heads(2, 1)
    for piece in os:
        piece.rest(0)
        piece.own(1)
    for piece in ws:
        piece.forward(0)
    heads(3, 2)
    for piece in os:
        piece.forward(1)
    for piece in ws:
        piece.rest(0)
        piece.own(1)
    heads(5, 2)
    for piece in os:
        piece.rest(1)
        piece.own(2)
        piece.to_near(0)
    heads(7, 3)
    for piece in ws:
        piece.forward(1)
    heads(10, 2)
    for piece in os:
        piece.forward(2)
    for piece in ws:
        piece.rest(1)
        piece.own(2)
        piece.to_near(0)
    for piece in os:
        piece.rest(2, far=False)
        piece.to_near(1)
        piece.to_near(3)
    for piece in os:
        piece.rest(2, sides=False)
        piece.to_near(2)
    for piece in os:
        for shift in range(4):
            piece.from_near(shift)
    loads[3].wait()

    def project(zz, _):
        rhs = jnp.concatenate(
            [
                jnp.concatenate(
                    [obuf[xx, zz, yh * 2 + l, cc] for xx in range(4) for yh in range(2) for cc in range(2)],
                    axis=0,
                )
                for l in range(2)
            ],
            axis=1,
        )
        cols = pl.ds(pl.multiple_of(zz * 768, 768), 768)
        proj = dot(qs[...], rhs)
        mix[:, cols] = (tok[:, cols].astype(F32) + mod[0, 0:1, cols] * proj).astype(BF)
        return 0

    lax.fori_loop(0, 4, project, 0)
    for piece in ws:
        piece.forward(2)

    def normed(t):
        rows = pl.ds(pl.multiple_of(t * 48, 16), 48)
        wide = mix[rows, :].astype(F32)
        mean = jnp.mean(wide, axis=1, keepdims=True)
        dev = wide - mean
        var = jnp.mean(dev * dev, axis=1, keepdims=True)
        return rows, (dev * lax.rsqrt(var + 1e-06) * (1.0 + mod[0, 2:3, :]) + mod[0, 1:2, :]).astype(BF)

    def norm_and_send(i, _):
        t = lax.rem(chip + 1 + i, 8)
        rows, value = normed(t)
        mix[rows, :] = value
        remote(mix.at[rows, :], moved.at[seq], a2a_s.at[i], a2a_r.at[i], other_chip(t)).start()
        return 0

    lax.fori_loop(0, 7, norm_and_send, 0)
    moved[seq] = normed(chip)[1]

    def to_near_rows(i):
        t = lax.rem(chip + 7 - i, 8)
        ref = moved.at[t * 2 + c, pl.ds(pl.multiple_of(16 * (1 - c), 16), 32), :]
        return remote(ref, ref, fwd_s.at[i], fwd_r.at[i], near)

    to_near_rows(7).start()

    def pass_on(i, _):
        t = lax.rem(chip + 7 - i, 8)
        ref = moved.at[t * 2 + c]
        remote(ref, ref, a2a_s.at[i], a2a_r.at[i], near).wait_recv()
        to_near_rows(i).start()
        return 0

    lax.fori_loop(0, 7, pass_on, 0)

    def arrive(i, _):
        t = lax.rem(chip + 7 - i, 8)
        ref = moved.at[t * 2 + 1 - c, pl.ds(pl.multiple_of(16 * c, 16), 32), :]
        remote(ref, ref, fwd_s.at[i], fwd_r.at[i], near).wait_recv()
        return 0

    lax.fori_loop(0, 8, arrive, 0)

    m = lax.broadcasted_iota(jnp.int32, (384, 512), 0)
    r = lax.broadcasted_iota(jnp.int32, (384, 512), 1)
    pick = (r == (m & 15) * 32 + (m >> 4) + 8 * c).astype(F32).astype(BF)

    def turn(i, _):
        cols = pl.ds(pl.multiple_of(i * 384, 384), 384)
        rows = moved[:, pl.ds(pl.multiple_of(16 * c, 16), 32), cols].reshape(512, 384)
        xt[cols, :] = dot(pick, rows).astype(BF).T
        return 0

    lax.fori_loop(0, 8, turn, 0)

    def put(rows, value, first):
        if first:
            acc[rows, :] = value
        else:
            acc[rows, :] += value

    def start_row(zz, l, cc, r0):
        return pl.multiple_of(zz * 1152 + l * 576 + cc * 288 + r0, 16)

    def chunk_x(shift):
        _, r0, n, _ = W_PIECES[0]
        xx = lax.rem(x + shift, 4)
        rhs_rows = pl.ds(pl.multiple_of(xx * 768, 768), 768)

        def body(zz, _):
            lhs = jnp.concatenate(
                [
                    jnp.concatenate([wbuf[xx, zz, yh * 2 + l, cc, r0 : r0 + n, :] for yh in range(2)], axis=1)
                    for l in range(2)
                    for cc in range(2)
                ],
                axis=0,
            )
            res = dot(lhs, xt[rhs_rows, :])
            for i in range(4):
                put(pl.ds(start_row(zz, i // 2, i % 2, r0), n), res[i * n : (i + 1) * n], shift == 0)
            return 0

        lax.fori_loop(0, 4, body, 0)

    def chunk_y(shift, first):
        _, r0, n, _ = W_PIECES[1]
        yy = lax.rem(y + shift, 4)
        hi, lo = yy // 2, yy % 2
        rhs = jnp.concatenate(
            [xt[pl.ds(pl.multiple_of(xx * 768 + hi * 384, 384), 384), :] for xx in range(4)], axis=0
        )

        def body(zp, _):
            lhs = jnp.concatenate(
                [
                    jnp.concatenate([wbuf[xx, zp * 2 + zz, yy, cc, r0 : r0 + n, :] for xx in range(4)], axis=1)
                    for zz in range(2)
                    for cc in range(2)
                ],
                axis=0,
            )
            res = dot(lhs, rhs)
            for i in range(4):
                put(pl.ds(start_row(zp * 2 + i // 2, lo, i % 2, r0), n), res[i * n : (i + 1) * n], first)
            return 0

        lax.fori_loop(0, 2, body, 0)

    def chunk_z(shift):
        _, r0, n, _ = W_PIECES[2]
        zz = lax.rem(z + shift, 4)
        lhs = jnp.concatenate(
            [
                jnp.concatenate(
                    [wbuf[xx, zz, yh * 2 + l, cc, r0 : r0 + n, :] for xx in range(4) for yh in range(2)], axis=1
                )
                for l in range(2)
                for cc in range(2)
            ],
            axis=0,
        )
        res = dot(lhs, xt[...])
        for i in range(4):
            put(pl.ds(start_row(zz, i // 2, i % 2, r0), n), res[i * n : (i + 1) * n], True)

    def chunk(shift):
        for piece in ws:
            piece.from_near(shift)
        chunk_x(shift)
        chunk_y(shift, shift < 2)
        chunk_z(shift)

    chunk(0)
    for piece in ws:
        piece.rest(2, far=False)
        piece.to_near(1)
        piece.to_near(3)
    chunk(1)
    chunk(3)
    for piece in ws:
        piece.rest(2, sides=False)
        piece.to_near(2)
    chunk(2)

    def unit(rows, gain):
        wide = acc[rows, :].astype(BF).astype(F32)
        scale = lax.rsqrt(jnp.sum(wide * wide, axis=0, keepdims=True) * (1.0 / 128) + 1e-06)
        return (wide * scale * gain).astype(BF)

    ii = lax.broadcasted_iota(jnp.int32, (128, 128), 0)
    jj = lax.broadcasted_iota(jnp.int32, (128, 128), 1)
    same = (ii >> 4) == (jj >> 4)

    def temporal(h, _):
        rows = pl.multiple_of(h * 128, 128)
        q = unit(pl.ds(rows, 128), qg[...])
        k = unit(pl.ds(1536 + rows, 128), kg[...])
        v = acc[pl.ds(3072 + rows, 128), :].astype(BF)
        for g in range(3):
            cols = slice(g * 128, (g + 1) * 128)
            s = dot(k[:, cols].T, q[:, cols]) * (128**-0.5)
            s = jnp.where(same, s, -1e30)
            e = jnp.exp(s - jnp.max(s, axis=0, keepdims=True))
            p = (e / jnp.sum(e, axis=0, keepdims=True)).astype(BF)
            ot[pl.ds(rows, 128), cols] = dot(v[:, cols], p).astype(BF)
        return 0

    lax.fori_loop(0, 12, temporal, 0)

    a = lax.broadcasted_iota(jnp.int32, (384, 384), 0)
    b = lax.broadcasted_iota(jnp.int32, (384, 384), 1)
    back = (a == (b & 15) * 24 + (b >> 4)).astype(F32).astype(BF)

    def untangle(i, _):
        cols = pl.ds(pl.multiple_of(i * 384, 384), 384)
        ks[:, cols] = lax.dot_general(
            back, ot[cols, :], (((1,), (1,)), ((), ())), preferred_element_type=F32
        ).astype(BF)
        return 0

    lax.fori_loop(0, 4, untangle, 0)
    done = pltpu.make_async_copy(ks, out_hbm, out_sem)
    done.start()

    for copy in pending:
        copy.wait_send()

    def sent(i, _):
        t = lax.rem(chip + 1 + i, 8)
        rows = pl.ds(pl.multiple_of(t * 48, 16), 48)
        remote(mix.at[rows, :], moved.at[seq], a2a_s.at[i], a2a_r.at[i], other_chip(t)).wait_send()
        return 0

    lax.fori_loop(0, 7, sent, 0)

    def sent_near(i, _):
        to_near_rows(i).wait_send()
        return 0

    lax.fori_loop(0, 8, sent_near, 0)
    done.wait()


def local(
    tokens, spatial_query, spatial_key, spatial_value, out_weight, qkv_weight, modulation, query_gain, key_gain
):
    hbm = pl.BlockSpec(memory_space=pl.ANY)
    vmem = pl.BlockSpec(memory_space=pltpu.VMEM)
    dma = pltpu.SemaphoreType.DMA
    out = pl.pallas_call(
        kernel,
        out_shape=jax.ShapeDtypeStruct((384, 1536), BF),
        in_specs=[hbm] * 4 + [vmem] * 5,
        out_specs=hbm,
        scratch_shapes=[
            pltpu.VMEM((4, 4, 4, 2, 288, 384), BF),
            pltpu.VMEM((4, 4, 4, 2, 96, 384), BF),
            pltpu.VMEM((4608, 384), F32),
            pltpu.VMEM((384, 3072), BF),
            pltpu.VMEM((384, 1536), BF),
            pltpu.VMEM((384, 1536), BF),
            pltpu.VMEM((384, 1536), BF),
            pltpu.VMEM((384, 3072), BF),
            pltpu.VMEM((16, 48, 3072), BF),
            pltpu.VMEM((3072, 384), BF),
            pltpu.VMEM((1536, 384), BF),
            pltpu.VMEM((96, 192), BF),
            dma((4,)),
            dma,
            dma((18, 2, 3)),
            dma((18, 2, 3)),
            dma((6, 4)),
            dma((6, 4)),
            dma,
            dma,
            dma((7,)),
            dma((7,)),
            dma((8,)),
            dma((8,)),
        ],
        compiler_params=pltpu.CompilerParams(
            collective_id=0, has_side_effects=True, vmem_limit_bytes=64 * 2**20 - 65536 * 4
        ),
        name="video_block",
    )(
        spatial_query.reshape(384, 1536),
        spatial_key.reshape(384, 1536),
        spatial_value.reshape(384, 1536),
        tokens.reshape(384, 3072),
        out_weight,
        qkv_weight.T,
        modulation,
        query_gain.reshape(128, 1),
        key_gain.reshape(128, 1),
    )
    return out.reshape(1, 16, 24, 1536)


def solution(mesh):
    placed = (
        P("dp", "seq", None, None),
        P("dp", "seq", None, None),
        P("dp", "seq", None, None),
        P("dp", "seq", None, None),
        P("dp", "seq"),
        P("dp", "seq"),
        P("dp", None, None),
        P(),
        P(),
    )
    return jax.shard_map(
        local, mesh=mesh, in_specs=placed, out_specs=P("dp", None, "seq", None), check_vma=False
    )
```

```python
import functools

import jax
import jax.numpy as jnp
from jax import lax
from jax.experimental import pallas as pl
from jax.experimental.pallas import tpu as pltpu
from jax.sharding import PartitionSpec as P

MESH = pl.DeviceIdType.MESH
BF = jnp.bfloat16
F32 = jnp.float32

W_PIECES = (("yzx", 0, 128, 64), ("zxy", 128, 96, 48), ("xyz", 224, 64, 32))
O_PIECES = (("yzx", 0, 32, 16), ("zxy", 32, 32, 16), ("xyz", 64, 32, 16))


def dot(a, b):
    return jnp.dot(a, b, preferred_element_type=F32)


def kernel(
    q_hbm, k_hbm, v_hbm, tok_hbm, ow_hbm, wt_hbm, mod_hbm, qg_hbm, kg_hbm, ot,
    ow, mods, mod, qg, kg, wbuf, obuf, acc, tok, qs, ks, vs, mix, moved, xt, oin,
    load_sem, ring_s, ring_r, near_s, near_r, oin_s, oin_r, a2a_s, a2a_r, fwd_s, fwd_r,
):
    dp = lax.axis_index("dp")
    seq = lax.axis_index("seq")
    x, z, c = dp // 2, seq // 4, seq % 2
    yl = (seq // 2) % 2
    y = (dp % 2) * 2 + yl
    me = {"x": x, "y": y, "z": z}
    chip = z * 2 + yl

    def device(at, core):
        return (at["x"] * 2 + at["y"] // 2, at["z"] * 4 + (at["y"] % 2) * 2 + core)

    def step(axis, by):
        return {**me, axis: lax.rem(me[axis] + by, 4)}

    def other_chip(t):
        return (dp, t * 2 + c)

    near = device(me, 1 - c)

    parts = (
        (ow_hbm, ow), (wt_hbm, wbuf.at[x, z, y, c]), (q_hbm, qs), (k_hbm, ks), (v_hbm, vs), (tok_hbm, tok),
        (mod_hbm, mods), (qg_hbm, qg), (kg_hbm, kg),
    )
    loads = [pltpu.make_async_copy(src, dst, load_sem.at[i]) for i, (src, dst) in enumerate(parts)]
    for copy in loads:
        copy.start()

    barrier = pltpu.get_barrier_semaphore()
    partners = [device(step(a, by), c) for a in "xyz" for by in (1, 2, 3)] + [near]
    flip = z * 2 + (1 - yl)
    partners += [other_chip(lax.rem(flip + 2 * k, 8)) for k in (1, 2, 3)]
    for partner in partners:
        pl.semaphore_signal(barrier, inc=1, device_id=partner, device_id_type=MESH)
    pl.semaphore_wait(barrier, len(partners))
    loads[0].wait()
    loads[1].wait()

    pending = []

    def remote(src, dst, send, recv, to):
        return pltpu.make_async_remote_copy(
            src_ref=src, dst_ref=dst, send_sem=send, recv_sem=recv, device_id=to, device_id_type=MESH
        )

    def start(src, dst, send, recv, to):
        copy = remote(src, dst, send, recv, to)
        copy.start()
        pending.append(copy)

    def shift(axis, part):
        if axis == "y":
            return (0, 1 + 2 * yl, 3 - 2 * yl, 2)[part]
        return (0, 3, 1, 2)[part]

    def to(axis, way):
        by = (1 + 2 * yl, 3 - 2 * yl)[way] if axis == "y" else (1, 3)[way]
        return device(step(axis, by), c)

    class Piece:
        def __init__(self, buf, spec, base):
            self.buf = buf
            self.order, self.r0, self.n, self.half = spec
            self.base = base

        def slot(self, phase, part, rows="W", group=None, core=None):
            at = dict(me)
            for axis in self.order[:phase]:
                at[axis] = slice(None)
            axis = self.order[phase]
            at[axis] = lax.rem(me[axis] + shift(axis, part), 4)
            if group is not None:
                second = self.order[1]
                at[second] = lax.rem(me[second] + shift(second, group), 4)
            r0, n = {
                "A": (self.r0, self.half),
                "B": (self.r0 + self.half, self.n - self.half),
                "W": (self.r0, self.n),
            }[rows]
            return self.buf.at[at["x"], at["z"], at["y"], c if core is None else core, pl.ds(r0, n), :]

        def sem(self, i):
            return ring_s.at[self.base, i], ring_r.at[self.base, i]

        def send(self, ref, i, target):
            start(ref, ref, *self.sem(i), target)

        def wait(self, ref, i):
            remote(ref, ref, *self.sem(i), near).wait_recv()

        def first(self):
            axis = self.order[0]
            ref = self.slot(0, 0)
            self.send(ref, 0, to(axis, 0))
            self.send(ref, 1, to(axis, 1))
            self.send(ref, 2, device(step(axis, 2), c))

        def first_done(self):
            for part in (1, 2, 3):
                self.wait(self.slot(0, part), part - 1)

        def second(self):
            axis = self.order[1]
            for k in range(2):
                for way in range(2):
                    self.send(self.slot(1, 0, "AB"[(way + k) % 2]), 3 + way * 3 + k, to(axis, way))

        def second_on(self):
            axis = self.order[1]
            for way in range(2):
                came = 1 - way if axis == "y" else way
                ref = self.slot(1, 1 + came, "AB"[came])
                self.wait(ref, 3 + came * 3)
                self.send(ref, 3 + way * 3 + 2, to(axis, way))

        def second_sides(self):
            for way in range(2):
                self.wait(self.slot(1, 1 + way, "BA"[way]), 3 + way * 3 + 1)

        def second_far(self):
            axis = self.order[1]
            for way in range(2):
                came = 1 - way if axis == "y" else way
                self.wait(self.slot(1, 3, "AB"[came]), 3 + way * 3 + 2)

        def third(self, group):
            axis = self.order[2]
            for way in range(2):
                self.send(self.slot(2, 0, group=group), 9 + way * 4 + group, to(axis, way))

        def relays(self, way):
            if self.order[2] == "y":
                return ((), (0, 1, 2, 3))[way]
            return ((0, 1), (2, 3))[way]

        def third_on(self, group):
            axis = self.order[2]
            for way in range(2):
                came = 1 - way if axis == "y" else way
                ref = self.slot(2, 1 + came, group=group)
                self.wait(ref, 9 + came * 4 + group)
                if group in self.relays(way):
                    self.send(ref, 17 + way * 4 + group, to(axis, way))

        def third_far(self, group):
            way = 0 if group in self.relays(0) else 1
            self.wait(self.slot(2, 3, group=group), 17 + way * 4 + group)

        def across(self, part, group=None):
            i = part if group is None else 3 + group
            ref = self.slot(2, part, group=group)
            start(ref, ref, near_s.at[self.base, i], near_r.at[self.base, i], near)

        def crossed(self, part, group=None):
            i = part if group is None else 3 + group
            ref = self.slot(2, part, group=group, core=1 - c)
            remote(ref, ref, near_s.at[self.base, i], near_r.at[self.base, i], near).wait_recv()

    ws = [Piece(wbuf, spec, i) for i, spec in enumerate(W_PIECES)]
    os = [Piece(obuf, spec, 3 + i) for i, spec in enumerate(O_PIECES)]

    def each(pieces, name, *args):
        for piece in pieces:
            getattr(piece, name)(*args)

    half = ow.at[pl.ds(pl.multiple_of(96 * (1 - c), 16), 96), :]
    start(half, oin, oin_s, oin_r, near)
    each(ws, "first")
    row = lax.broadcasted_iota(jnp.int32, (192, 384), 0)
    col = lax.broadcasted_iota(jnp.int32, (192, 384), 1)
    mine = ow[pl.ds(pl.multiple_of(96 * c, 16), 96), :]
    block = dot(mine, (col - row == 192 * c).astype(F32).astype(BF))
    remote(oin, oin, oin_s, oin_r, near).wait_recv()
    block += dot(oin[...], (col - row == 192 * (1 - c)).astype(F32).astype(BF))
    obuf[x, z, y, c] = block.astype(BF)
    each(os, "first")

    for copy in loads[2:5]:
        copy.wait()

    def heads(first, count):
        def body(h, _):
            cols = pl.ds(pl.multiple_of(h * 128, 128), 128)
            s = lax.dot_general(
                qs[:, cols], ks[:, cols], (((1,), (1,)), ((), ())), preferred_element_type=F32
            )
            s = s * (128**-0.5)
            e = jnp.exp(s - jnp.max(s, axis=1, keepdims=True))
            total = jnp.sum(e, axis=1, keepdims=True)
            o = dot(e.astype(BF), vs[:, cols])
            qs[:, cols] = (o / total).astype(BF)
            return 0

        lax.fori_loop(first, first + count, body, 0)

    heads(0, 2)
    each(os, "first_done")
    each(os, "second")
    each(os, "third", 0)
    each(ws, "first_done")
    each(ws, "second")
    heads(2, 2)
    each(os, "second_on")
    heads(4, 2)
    each(os, "second_sides")
    each(os, "third", 1)
    each(os, "third", 2)
    each(ws, "second_on")
    heads(6, 2)
    each(os, "second_far")
    each(os, "third", 3)
    each(os, "across", 0)
    each(ws, "third", 0)
    heads(8, 2)
    each(os, "third_on", 0)
    heads(10, 2)
    each(os, "third_on", 1)
    each(os, "third_on", 2)
    each(ws, "second_sides")
    each(ws, "second_far")
    each(os, "third_on", 3)
    for group in (1, 2, 3):
        each(ws, "third", group)
    each(os, "across", 1)
    each(os, "across", 2)
    for group in range(4):
        each(os, "third_far", group)
        each(os, "across", 3, group)
    each(ws, "across", 0)
    for part in range(3):
        each(os, "crossed", part)
    for group in range(4):
        each(os, "crossed", 3, group)
    loads[5].wait()
    loads[6].wait()
    for i in range(72):
        mod[i // 24 : i // 24 + 1, i % 24 * 128 : (i % 24 + 1) * 128] = mods[i : i + 1, :]

    def project(zz, _):
        rhs = jnp.concatenate(
            [
                jnp.concatenate(
                    [obuf[xx, zz, yh * 2 + l, cc] for xx in range(4) for yh in range(2) for cc in range(2)],
                    axis=0,
                )
                for l in range(2)
            ],
            axis=1,
        )
        cols = pl.ds(pl.multiple_of(zz * 768, 768), 768)
        proj = dot(qs[...], rhs)
        mix[:, cols] = (tok[:, cols].astype(F32) + mod[0:1, cols] * proj).astype(BF)
        return 0

    lax.fori_loop(0, 4, project, 0)
    each(ws, "third_on", 0)

    def normed(t):
        rows = pl.ds(pl.multiple_of(t * 48, 16), 48)
        wide = mix[rows, :].astype(F32)
        mean = jnp.mean(wide, axis=1, keepdims=True)
        dev = wide - mean
        var = jnp.mean(dev * dev, axis=1, keepdims=True)
        return rows, (dev * lax.rsqrt(var + 1e-06) * (1.0 + mod[2:3, :]) + mod[1:2, :]).astype(BF)

    def norm_and_send(i, _):
        t = lax.rem(chip + 1 + i, 8)
        rows, value = normed(t)
        mix[rows, :] = value
        remote(mix.at[rows, :], moved.at[seq], a2a_s.at[i], a2a_r.at[i], other_chip(t)).start()
        return 0

    lax.fori_loop(0, 7, norm_and_send, 0)
    each(ws, "third_on", 1)
    each(ws, "third_on", 2)
    moved[seq] = normed(chip)[1]

    def to_near_rows(i):
        t = lax.rem(chip + 7 - i, 8)
        ref = moved.at[t * 2 + c, pl.ds(pl.multiple_of(16 * (1 - c), 16), 32), :]
        return remote(ref, ref, fwd_s.at[i], fwd_r.at[i], near)

    to_near_rows(7).start()
    each(ws, "third_on", 3)
    each(ws, "across", 1)
    each(ws, "across", 2)

    def pass_on(i, _):
        t = lax.rem(chip + 7 - i, 8)
        ref = moved.at[t * 2 + c]
        remote(ref, ref, a2a_s.at[i], a2a_r.at[i], near).wait_recv()
        to_near_rows(i).start()
        return 0

    lax.fori_loop(0, 7, pass_on, 0)

    def arrive(i, _):
        t = lax.rem(chip + 7 - i, 8)
        ref = moved.at[t * 2 + 1 - c, pl.ds(pl.multiple_of(16 * c, 16), 32), :]
        remote(ref, ref, fwd_s.at[i], fwd_r.at[i], near).wait_recv()
        return 0

    lax.fori_loop(0, 8, arrive, 0)

    m = lax.broadcasted_iota(jnp.int32, (384, 512), 0)
    r = lax.broadcasted_iota(jnp.int32, (384, 512), 1)
    pick = (r == (m & 15) * 32 + (m >> 4) + 8 * c).astype(F32).astype(BF)

    def turn(i, _):
        cols = pl.ds(pl.multiple_of(i * 384, 384), 384)
        rows = moved[:, pl.ds(pl.multiple_of(16 * c, 16), 32), cols].reshape(512, 384)
        xt[cols, :] = dot(pick, rows).astype(BF).T
        return 0

    lax.fori_loop(0, 8, turn, 0)

    def put(rows, value, first):
        if first:
            acc[rows, :] = value
        else:
            acc[rows, :] += value

    def start_row(zz, l, cc, r0):
        return pl.multiple_of(zz * 1152 + l * 576 + cc * 288 + r0, 16)

    def chunk_x(part):
        _, r0, n, _ = W_PIECES[0]
        xx = lax.rem(x + shift("x", part), 4)
        rhs_rows = pl.ds(pl.multiple_of(xx * 768, 768), 768)

        def body(zz, _):
            lhs = jnp.concatenate(
                [
                    jnp.concatenate([wbuf[xx, zz, yh * 2 + l, cc, r0 : r0 + n, :] for yh in range(2)], axis=1)
                    for l in range(2)
                    for cc in range(2)
                ],
                axis=0,
            )
            res = dot(lhs, xt[rhs_rows, :])
            for i in range(4):
                put(pl.ds(start_row(zz, i // 2, i % 2, r0), n), res[i * n : (i + 1) * n], part == 0)
            return 0

        lax.fori_loop(0, 4, body, 0)

    def chunk_y(part):
        first = part < 2
        _, r0, n, _ = W_PIECES[1]
        yy = lax.rem(y + shift("y", part), 4)
        hi, lo = yy // 2, yy % 2
        rhs = jnp.concatenate(
            [xt[pl.ds(pl.multiple_of(xx * 768 + hi * 384, 384), 384), :] for xx in range(4)], axis=0
        )

        def body(zp, _):
            lhs = jnp.concatenate(
                [
                    jnp.concatenate([wbuf[xx, zp * 2 + zz, yy, cc, r0 : r0 + n, :] for xx in range(4)], axis=1)
                    for zz in range(2)
                    for cc in range(2)
                ],
                axis=0,
            )
            res = dot(lhs, rhs)
            for i in range(4):
                put(pl.ds(start_row(zp * 2 + i // 2, lo, i % 2, r0), n), res[i * n : (i + 1) * n], first)
            return 0

        lax.fori_loop(0, 2, body, 0)

    def chunk_z(part):
        _, r0, n, _ = W_PIECES[2]
        zz = lax.rem(z + shift("z", part), 4)
        lhs = jnp.concatenate(
            [
                jnp.concatenate(
                    [wbuf[xx, zz, yh * 2 + l, cc, r0 : r0 + n, :] for xx in range(4) for yh in range(2)], axis=1
                )
                for l in range(2)
                for cc in range(2)
            ],
            axis=0,
        )
        res = dot(lhs, xt[...])
        for i in range(4):
            put(pl.ds(start_row(zz, i // 2, i % 2, r0), n), res[i * n : (i + 1) * n], True)

    def chunk(part):
        chunk_x(part)
        chunk_y(part)
        chunk_z(part)

    each(ws, "crossed", 0)
    chunk(0)
    each(ws, "crossed", 1)
    chunk(1)
    each(ws, "third_far", 0)
    each(ws, "across", 3, 0)
    each(ws, "crossed", 2)
    chunk(2)
    for group in (1, 2, 3):
        each(ws, "third_far", group)
        each(ws, "across", 3, group)
    for group in range(4):
        each(ws, "crossed", 3, group)
    chunk(3)
    loads[7].wait()
    loads[8].wait()

    def unit(rows, gain):
        wide = acc[rows, :].astype(BF).astype(F32)
        scale = lax.rsqrt(jnp.sum(wide * wide, axis=0, keepdims=True) * (1.0 / 128) + 1e-06)
        return (wide * scale * gain).astype(BF)

    def column(gain):
        return jnp.concatenate([jnp.broadcast_to(gain[...], (128, 128)).T] * 3, axis=1)

    qcol, kcol = column(qg), column(kg)
    ii = lax.broadcasted_iota(jnp.int32, (128, 128), 0)
    jj = lax.broadcasted_iota(jnp.int32, (128, 128), 1)
    same = (ii >> 4) == (jj >> 4)

    def temporal(h, _):
        rows = pl.multiple_of(h * 128, 128)
        q = unit(pl.ds(rows, 128), qcol)
        k = unit(pl.ds(1536 + rows, 128), kcol)
        v = acc[pl.ds(3072 + rows, 128), :].astype(BF)
        for g in range(3):
            cols = slice(g * 128, (g + 1) * 128)
            s = dot(k[:, cols].T, q[:, cols]) * (128**-0.5)
            s = jnp.where(same, s, -1e30)
            e = jnp.exp(s - jnp.max(s, axis=0, keepdims=True))
            p = (e / jnp.sum(e, axis=0, keepdims=True)).astype(BF)
            ot[pl.ds(rows, 128), cols] = dot(v[:, cols], p).astype(BF)
        return 0

    lax.fori_loop(0, 12, temporal, 0)

    for copy in pending:
        copy.wait_send()

    def sent(i, _):
        t = lax.rem(chip + 1 + i, 8)
        rows = pl.ds(pl.multiple_of(t * 48, 16), 48)
        remote(mix.at[rows, :], moved.at[seq], a2a_s.at[i], a2a_r.at[i], other_chip(t)).wait_send()
        return 0

    lax.fori_loop(0, 7, sent, 0)

    def sent_near(i, _):
        to_near_rows(i).wait_send()
        return 0

    lax.fori_loop(0, 8, sent_near, 0)


def untangle(ot, out):
    a = lax.broadcasted_iota(jnp.int32, (128, 384), 0) + pl.program_id(0) * 128
    b = lax.broadcasted_iota(jnp.int32, (128, 384), 1)
    back = (a == (b & 15) * 24 + (b >> 4)).astype(F32).astype(BF)
    out[...] = lax.dot_general(back, ot[...], (((1,), (1,)), ((), ())), preferred_element_type=F32).astype(BF)


def local(
    tokens, spatial_query, spatial_key, spatial_value, out_weight, qkv_weight, modulation, query_gain, key_gain
):
    hbm = pl.BlockSpec(memory_space=pl.ANY)
    dma = pltpu.SemaphoreType.DMA
    turned = pl.pallas_call(
        kernel,
        out_shape=jax.ShapeDtypeStruct((1536, 384), BF),
        in_specs=[hbm] * 9,
        out_specs=pl.BlockSpec(memory_space=pltpu.VMEM),
        scratch_shapes=[
            pltpu.VMEM((192, 192), BF),
            pltpu.VMEM((72, 128), F32),
            pltpu.VMEM((8, 3072), F32),
            pltpu.VMEM((1, 128), F32),
            pltpu.VMEM((1, 128), F32),
            pltpu.VMEM((4, 4, 4, 2, 288, 384), BF),
            pltpu.VMEM((4, 4, 4, 2, 96, 384), BF),
            pltpu.VMEM((4608, 384), F32),
            pltpu.VMEM((384, 3072), BF),
            pltpu.VMEM((384, 1536), BF),
            pltpu.VMEM((384, 1536), BF),
            pltpu.VMEM((384, 1536), BF),
            pltpu.VMEM((384, 3072), BF),
            pltpu.VMEM((16, 48, 3072), BF),
            pltpu.VMEM((3072, 384), BF),
            pltpu.VMEM((96, 192), BF),
            dma((9,)),
            dma((6, 25)),
            dma((6, 25)),
            dma((6, 7)),
            dma((6, 7)),
            dma,
            dma,
            dma((7,)),
            dma((7,)),
            dma((8,)),
            dma((8,)),
        ],
        compiler_params=pltpu.CompilerParams(
            collective_id=0, has_side_effects=True, vmem_limit_bytes=62 * 2**20
        ),
        name="video_block",
    )(
        spatial_query.reshape(384, 1536),
        spatial_key.reshape(384, 1536),
        spatial_value.reshape(384, 1536),
        tokens.reshape(384, 3072),
        out_weight,
        qkv_weight.T,
        modulation.reshape(72, 128),
        query_gain.reshape(1, 128),
        key_gain.reshape(1, 128),
    )
    out = pl.pallas_call(
        untangle,
        out_shape=jax.ShapeDtypeStruct((384, 1536), BF),
        grid=(3,),
        in_specs=[pl.BlockSpec(memory_space=pltpu.VMEM)],
        out_specs=pl.BlockSpec((128, 1536), lambda i: (i, 0)),
        name="frame_major",
    )(turned)
    return out.reshape(1, 16, 24, 1536)


def solution(mesh):
    placed = (
        P("dp", "seq", None, None),
        P("dp", "seq", None, None),
        P("dp", "seq", None, None),
        P("dp", "seq", None, None),
        P("dp", "seq"),
        P("dp", "seq"),
        P("dp", None, None),
        P(),
        P(),
    )
    return jax.shard_map(
        local, mesh=mesh, in_specs=placed, out_specs=P("dp", None, "seq", None), check_vma=False
    )
```

```python
import functools

import jax
import jax.numpy as jnp
from jax import lax
from jax.experimental import pallas as pl
from jax.experimental.pallas import tpu as pltpu
from jax.sharding import PartitionSpec as P

MESH = pl.DeviceIdType.MESH
BF = jnp.bfloat16
F32 = jnp.float32

W_PIECES = (("yzx", 0, 128, 64), ("zxy", 128, 96, 48), ("xyz", 224, 64, 32))
O_PIECES = (("yzx", 0, 32, 16), ("zxy", 32, 32, 16), ("xyz", 64, 32, 16))


def dot(a, b):
    return jnp.dot(a, b, preferred_element_type=F32)


def kernel(
    q_hbm, k_hbm, v_hbm, tok_hbm, ow_hbm, wt_hbm, mod_hbm, qg_hbm, kg_hbm, ot,
    ow, mods, mod, qg, kg, wbuf, obuf, acc, tok, qs, ks, vs, mix, moved, xt, oin,
    load_sem, ring_s, ring_r, near_s, near_r, oin_s, oin_r, a2a_s, a2a_r, fwd_s, fwd_r,
):
    dp = lax.axis_index("dp")
    seq = lax.axis_index("seq")
    x, z, c = dp // 2, seq // 4, seq % 2
    yl = (seq // 2) % 2
    y = (dp % 2) * 2 + yl
    me = {"x": x, "y": y, "z": z}
    chip = z * 2 + yl

    def device(at, core):
        return (at["x"] * 2 + at["y"] // 2, at["z"] * 4 + (at["y"] % 2) * 2 + core)

    def step(axis, by):
        return {**me, axis: lax.rem(me[axis] + by, 4)}

    def other_chip(t):
        return (dp, t * 2 + c)

    near = device(me, 1 - c)

    parts = (
        (ow_hbm, ow), (wt_hbm, wbuf.at[x, z, y, c]), (q_hbm, qs), (k_hbm, ks), (v_hbm, vs), (tok_hbm, tok),
        (mod_hbm, mods), (qg_hbm, qg), (kg_hbm, kg),
    )
    loads = [pltpu.make_async_copy(src, dst, load_sem.at[i]) for i, (src, dst) in enumerate(parts)]
    for copy in loads:
        copy.start()

    barrier = pltpu.get_barrier_semaphore()
    partners = [device(step(a, by), c) for a in "xyz" for by in (1, 2, 3)] + [near]
    flip = z * 2 + (1 - yl)
    partners += [other_chip(lax.rem(flip + 2 * k, 8)) for k in (1, 2, 3)]
    for partner in partners:
        pl.semaphore_signal(barrier, inc=1, device_id=partner, device_id_type=MESH)
    pl.semaphore_wait(barrier, len(partners))
    loads[0].wait()
    loads[1].wait()

    pending = []

    def remote(src, dst, send, recv, to):
        return pltpu.make_async_remote_copy(
            src_ref=src, dst_ref=dst, send_sem=send, recv_sem=recv, device_id=to, device_id_type=MESH
        )

    def start(src, dst, send, recv, to):
        copy = remote(src, dst, send, recv, to)
        copy.start()
        pending.append(copy)

    def shift(axis, part):
        if axis == "y":
            return (0, 1 + 2 * yl, 3 - 2 * yl, 2)[part]
        return (0, 3, 1, 2)[part]

    def to(axis, way):
        by = (1 + 2 * yl, 3 - 2 * yl)[way] if axis == "y" else (1, 3)[way]
        return device(step(axis, by), c)

    class Piece:
        def __init__(self, buf, spec, base):
            self.buf = buf
            self.order, self.r0, self.n, self.half = spec
            self.base = base

        def slot(self, phase, part, rows="W", group=None, core=None):
            at = dict(me)
            for axis in self.order[:phase]:
                at[axis] = slice(None)
            axis = self.order[phase]
            at[axis] = lax.rem(me[axis] + shift(axis, part), 4)
            if group is not None:
                second = self.order[1]
                at[second] = lax.rem(me[second] + shift(second, group), 4)
            r0, n = {
                "A": (self.r0, self.half),
                "B": (self.r0 + self.half, self.n - self.half),
                "W": (self.r0, self.n),
            }[rows]
            return self.buf.at[at["x"], at["z"], at["y"], c if core is None else core, pl.ds(r0, n), :]

        def sem(self, i):
            return ring_s.at[self.base, i], ring_r.at[self.base, i]

        def send(self, ref, i, target):
            start(ref, ref, *self.sem(i), target)

        def wait(self, ref, i):
            remote(ref, ref, *self.sem(i), near).wait_recv()

        def first(self):
            axis = self.order[0]
            ref = self.slot(0, 0)
            self.send(ref, 0, to(axis, 0))
            self.send(ref, 1, to(axis, 1))
            self.send(ref, 2, device(step(axis, 2), c))

        def first_done(self):
            for part in (1, 2, 3):
                self.wait(self.slot(0, part), part - 1)

        def second(self, k):
            axis = self.order[1]
            for way in range(2):
                    self.send(self.slot(1, 0, "AB"[(way + k) % 2]), 3 + way * 3 + k, to(axis, way))

        def second_on(self):
            axis = self.order[1]
            for way in range(2):
                came = 1 - way if axis == "y" else way
                ref = self.slot(1, 1 + came, "AB"[came])
                self.wait(ref, 3 + came * 3)
                self.send(ref, 3 + way * 3 + 2, to(axis, way))

        def second_sides(self):
            for way in range(2):
                self.wait(self.slot(1, 1 + way, "BA"[way]), 3 + way * 3 + 1)

        def second_far(self):
            axis = self.order[1]
            for way in range(2):
                came = 1 - way if axis == "y" else way
                self.wait(self.slot(1, 3, "AB"[came]), 3 + way * 3 + 2)

        def third(self, group):
            axis = self.order[2]
            for way in range(2):
                self.send(self.slot(2, 0, group=group), 9 + way * 4 + group, to(axis, way))

        def relays(self, way):
            if self.order[2] == "y":
                return ((), (0, 1, 2, 3))[way]
            return ((0, 1), (2, 3))[way]

        def third_on(self, group):
            axis = self.order[2]
            for way in range(2):
                came = 1 - way if axis == "y" else way
                ref = self.slot(2, 1 + came, group=group)
                self.wait(ref, 9 + came * 4 + group)
                if group in self.relays(way):
                    self.send(ref, 17 + way * 4 + group, to(axis, way))

        def third_far(self, group):
            way = 0 if group in self.relays(0) else 1
            self.wait(self.slot(2, 3, group=group), 17 + way * 4 + group)

        def across(self, part, group=None):
            i = part if group is None else 3 + group
            ref = self.slot(2, part, group=group)
            start(ref, ref, near_s.at[self.base, i], near_r.at[self.base, i], near)

        def crossed(self, part, group=None):
            i = part if group is None else 3 + group
            ref = self.slot(2, part, group=group, core=1 - c)
            remote(ref, ref, near_s.at[self.base, i], near_r.at[self.base, i], near).wait_recv()

    ws = [Piece(wbuf, spec, i) for i, spec in enumerate(W_PIECES)]
    os = [Piece(obuf, spec, 3 + i) for i, spec in enumerate(O_PIECES)]

    def each(pieces, name, *args):
        for piece in pieces:
            getattr(piece, name)(*args)

    half = ow.at[pl.ds(pl.multiple_of(96 * (1 - c), 16), 96), :]
    start(half, oin, oin_s, oin_r, near)
    each(ws, "first")
    row = lax.broadcasted_iota(jnp.int32, (192, 384), 0)
    col = lax.broadcasted_iota(jnp.int32, (192, 384), 1)
    mine = ow[pl.ds(pl.multiple_of(96 * c, 16), 96), :]
    block = dot(mine, (col - row == 192 * c).astype(F32).astype(BF))
    remote(oin, oin, oin_s, oin_r, near).wait_recv()
    block += dot(oin[...], (col - row == 192 * (1 - c)).astype(F32).astype(BF))
    obuf[x, z, y, c] = block.astype(BF)
    each(os, "first")

    for copy in loads[2:5]:
        copy.wait()

    def heads(first, count):
        def body(h, _):
            cols = pl.ds(pl.multiple_of(h * 128, 128), 128)
            s = lax.dot_general(
                qs[:, cols], ks[:, cols], (((1,), (1,)), ((), ())), preferred_element_type=F32
            )
            s = s * (128**-0.5)
            e = jnp.exp(s - jnp.max(s, axis=1, keepdims=True))
            total = jnp.sum(e, axis=1, keepdims=True)
            o = dot(e.astype(BF), vs[:, cols])
            qs[:, cols] = (o / total).astype(BF)
            return 0

        lax.fori_loop(first, first + count, body, 0)

    heads(0, 2)
    each(os, "first_done")
    each(os, "second", 0)
    each(os, "second", 1)
    each(os, "third", 0)
    each(ws, "first_done")
    heads(2, 2)
    each(os, "second_on")
    heads(4, 3)
    each(os, "second_sides")
    each(os, "third", 1)
    each(os, "third", 2)
    heads(7, 2)
    each(os, "second_far")
    each(os, "third", 3)
    each(os, "across", 0)
    each(ws, "second", 0)
    each(ws, "second", 1)
    heads(9, 3)
    each(os, "third_on", 0)
    each(ws, "third", 0)
    each(os, "third_on", 1)
    each(os, "third_on", 2)
    each(os, "third_on", 3)
    each(os, "across", 1)
    each(os, "across", 2)
    each(ws, "second_on")
    for group in range(4):
        each(os, "third_far", group)
        each(os, "across", 3, group)
    each(ws, "second_sides")
    each(ws, "third", 1)
    each(ws, "third", 2)
    for part in range(3):
        each(os, "crossed", part)
    for group in range(4):
        each(os, "crossed", 3, group)
    loads[5].wait()
    loads[6].wait()
    for i in range(72):
        mod[i // 24 : i // 24 + 1, i % 24 * 128 : (i % 24 + 1) * 128] = mods[i : i + 1, :]

    def project(zz, _):
        rhs = jnp.concatenate(
            [
                jnp.concatenate(
                    [obuf[xx, zz, yh * 2 + l, cc] for xx in range(4) for yh in range(2) for cc in range(2)],
                    axis=0,
                )
                for l in range(2)
            ],
            axis=1,
        )
        cols = pl.ds(pl.multiple_of(zz * 768, 768), 768)
        proj = dot(qs[...], rhs)
        mix[zz] = (tok[:, cols].astype(F32) + mod[0:1, cols] * proj).astype(BF)
        return 0

    lax.fori_loop(0, 4, project, 0)
    each(ws, "second_far")
    each(ws, "third", 3)
    each(ws, "across", 0)
    each(ws, "third_on", 0)

    def normed(t):
        rows = pl.ds(pl.multiple_of(t * 48, 16), 48)
        wide = jnp.concatenate([mix[i, rows, :] for i in range(4)], axis=1).astype(F32)
        mean = jnp.mean(wide, axis=1, keepdims=True)
        dev = wide - mean
        var = jnp.mean(dev * dev, axis=1, keepdims=True)
        return rows, (dev * lax.rsqrt(var + 1e-06) * (1.0 + mod[2:3, :]) + mod[1:2, :]).astype(BF)

    def norm(i, _):
        rows, value = normed(i)
        for block in range(4):
            mix[block, rows, :] = value[:, block * 768 : (block + 1) * 768]
        return 0

    lax.fori_loop(0, 8, norm, 0)

    def features(block):
        return lax.rem(x + shift("x", block), 4)

    def leave(block, i):
        t = lax.rem(chip + 1 + i, 8)
        rows = pl.ds(pl.multiple_of(t * 48, 16), 48)
        src, dst = mix.at[features(block), rows, :], moved.at[features(block), seq]
        return remote(src, dst, a2a_s.at[block, i], a2a_r.at[block, i], other_chip(t))

    def over(block, i, core):
        t = lax.rem(chip + 7 - i, 8)
        rows = pl.ds(pl.multiple_of(16 * (1 - core), 16), 32)
        ref = moved.at[features(block), t * 2 + core, rows, :]
        return remote(ref, ref, fwd_s.at[block, i], fwd_r.at[block, i], near)

    def times(count, body):
        def run(i, _):
            body(i)
            return 0

        lax.fori_loop(0, count, run, 0)

    for block in range(4):
        times(7, lambda i: leave(block, i).start())
    for block in range(4):
        moved[block, seq] = mix[block, pl.ds(pl.multiple_of(chip * 48, 16), 48), :]
    for block in range(4):
        over(block, 7, c).start()

    m = lax.broadcasted_iota(jnp.int32, (384, 512), 0)
    r = lax.broadcasted_iota(jnp.int32, (384, 512), 1)
    pick = (r == (m & 15) * 32 + (m >> 4) + 8 * c).astype(F32).astype(BF)

    def gather_block(block):
        def one(i):
            t = lax.rem(chip + 7 - i, 8)
            ref = moved.at[features(block), t * 2 + c]
            remote(ref, ref, a2a_s.at[block, i], a2a_r.at[block, i], near).wait_recv()
            over(block, i, c).start()

        times(7, one)
        times(8, lambda i: over(block, i, 1 - c).wait_recv())

        def turn(i):
            inner = pl.ds(pl.multiple_of(i * 384, 384), 384)
            rows = moved[features(block), :, pl.ds(pl.multiple_of(16 * c, 16), 32), inner].reshape(512, 384)
            at = pl.ds(pl.multiple_of(features(block) * 768 + i * 384, 384), 384)
            xt[at, :] = dot(pick, rows).astype(BF).T

        times(2, turn)

    def put(rows, value, first):
        if first:
            acc[rows, :] = value
        else:
            acc[rows, :] += value

    def start_row(zz, l, cc, r0):
        return pl.multiple_of(zz * 1152 + l * 576 + cc * 288 + r0, 16)

    def chunk_x(part, group=None):
        _, r0, n, _ = W_PIECES[0]
        xx = lax.rem(x + shift("x", part), 4)
        rhs_rows = pl.ds(pl.multiple_of(xx * 768, 768), 768)

        def body(zz, _):
            lhs = jnp.concatenate(
                [
                    jnp.concatenate([wbuf[xx, zz, yh * 2 + l, cc, r0 : r0 + n, :] for yh in range(2)], axis=1)
                    for l in range(2)
                    for cc in range(2)
                ],
                axis=0,
            )
            res = dot(lhs, xt[rhs_rows, :])
            for i in range(4):
                put(pl.ds(start_row(zz, i // 2, i % 2, r0), n), res[i * n : (i + 1) * n], part == 0)
            return 0

        if group is None:
            lax.fori_loop(0, 4, body, 0)
        else:
            body(lax.rem(z + shift("z", group), 4), 0)

    def chunk_y(part):
        first = part < 2
        _, r0, n, _ = W_PIECES[1]
        yy = lax.rem(y + shift("y", part), 4)
        hi, lo = yy // 2, yy % 2
        rhs = jnp.concatenate(
            [xt[pl.ds(pl.multiple_of(xx * 768 + hi * 384, 384), 384), :] for xx in range(4)], axis=0
        )

        def body(zp, _):
            lhs = jnp.concatenate(
                [
                    jnp.concatenate([wbuf[xx, zp * 2 + zz, yy, cc, r0 : r0 + n, :] for xx in range(4)], axis=1)
                    for zz in range(2)
                    for cc in range(2)
                ],
                axis=0,
            )
            res = dot(lhs, rhs)
            for i in range(4):
                put(pl.ds(start_row(zp * 2 + i // 2, lo, i % 2, r0), n), res[i * n : (i + 1) * n], first)
            return 0

        lax.fori_loop(0, 2, body, 0)

    def chunk_z(part):
        _, r0, n, _ = W_PIECES[2]
        zz = lax.rem(z + shift("z", part), 4)
        lhs = jnp.concatenate(
            [
                jnp.concatenate(
                    [wbuf[xx, zz, yh * 2 + l, cc, r0 : r0 + n, :] for xx in range(4) for yh in range(2)], axis=1
                )
                for l in range(2)
                for cc in range(2)
            ],
            axis=0,
        )
        res = dot(lhs, xt[...])
        for i in range(4):
            put(pl.ds(start_row(zz, i // 2, i % 2, r0), n), res[i * n : (i + 1) * n], True)

    each(ws, "third_on", 1)
    each(ws, "third_on", 2)
    gather_block(0)
    each(ws, "crossed", 0)
    chunk_x(0)
    each(ws, "third_on", 3)
    each(ws, "across", 1)
    each(ws, "across", 2)
    gather_block(1)
    each(ws, "crossed", 1)
    chunk_x(1)
    gather_block(2)
    each(ws, "crossed", 2)
    chunk_x(2)
    each(ws, "third_far", 0)
    each(ws, "across", 3, 0)
    gather_block(3)
    chunk_y(0)
    chunk_z(0)
    each(ws, "third_far", 1)
    each(ws, "across", 3, 1)
    chunk_y(1)
    chunk_z(1)
    each(ws, "third_far", 2)
    each(ws, "across", 3, 2)
    chunk_y(2)
    chunk_z(2)
    each(ws, "third_far", 3)
    each(ws, "across", 3, 3)
    for group in range(3):
        each(ws[:1], "crossed", 3, group)
        chunk_x(3, group)
    for group in range(4):
        each(ws[1:], "crossed", 3, group)
    chunk_y(3)
    chunk_z(3)
    each(ws[:1], "crossed", 3, 3)
    chunk_x(3, 3)
    loads[7].wait()
    loads[8].wait()

    def unit(rows, gain):
        wide = acc[rows, :].astype(BF).astype(F32)
        scale = lax.rsqrt(jnp.sum(wide * wide, axis=0, keepdims=True) * (1.0 / 128) + 1e-06)
        return (wide * scale * gain).astype(BF)

    def column(gain):
        return jnp.concatenate([jnp.broadcast_to(gain[...], (128, 128)).T] * 3, axis=1)

    qcol, kcol = column(qg), column(kg)
    ii = lax.broadcasted_iota(jnp.int32, (128, 128), 0)
    jj = lax.broadcasted_iota(jnp.int32, (128, 128), 1)
    same = (ii >> 4) == (jj >> 4)

    def temporal(h):
        rows = pl.multiple_of(h * 128, 128)
        q = unit(pl.ds(rows, 128), qcol)
        k = unit(pl.ds(1536 + rows, 128), kcol)
        v = acc[pl.ds(3072 + rows, 128), :].astype(BF)
        for g in range(3):
            cols = slice(g * 128, (g + 1) * 128)
            s = dot(k[:, cols].T, q[:, cols]) * (128**-0.5)
            s = jnp.where(same, s, -1e30)
            e = jnp.exp(s - jnp.max(s, axis=0, keepdims=True))
            p = (e / jnp.sum(e, axis=0, keepdims=True)).astype(BF)
            ot[pl.ds(rows, 128), cols] = dot(v[:, cols], p).astype(BF)

    def two_heads(i, _):
        temporal(i * 2)
        temporal(i * 2 + 1)
        return 0

    lax.fori_loop(0, 6, two_heads, 0)

    for copy in pending:
        copy.wait_send()

    for block in range(4):
        times(7, lambda i: leave(block, i).wait_send())
        times(8, lambda i: over(block, i, c).wait_send())


def untangle(ot, out):
    a = lax.broadcasted_iota(jnp.int32, (128, 384), 0) + pl.program_id(0) * 128
    b = lax.broadcasted_iota(jnp.int32, (128, 384), 1)
    back = (a == (b & 15) * 24 + (b >> 4)).astype(F32).astype(BF)
    out[...] = lax.dot_general(back, ot[...], (((1,), (1,)), ((), ())), preferred_element_type=F32).astype(BF)


def local(
    tokens, spatial_query, spatial_key, spatial_value, out_weight, qkv_weight, modulation, query_gain, key_gain
):
    hbm = pl.BlockSpec(memory_space=pl.ANY)
    dma = pltpu.SemaphoreType.DMA
    turned = pl.pallas_call(
        kernel,
        out_shape=jax.ShapeDtypeStruct((1536, 384), BF),
        in_specs=[hbm] * 9,
        out_specs=pl.BlockSpec(memory_space=pltpu.VMEM),
        scratch_shapes=[
            pltpu.VMEM((192, 192), BF),
            pltpu.VMEM((72, 128), F32),
            pltpu.VMEM((8, 3072), F32),
            pltpu.VMEM((1, 128), F32),
            pltpu.VMEM((1, 128), F32),
            pltpu.VMEM((4, 4, 4, 2, 288, 384), BF),
            pltpu.VMEM((4, 4, 4, 2, 96, 384), BF),
            pltpu.VMEM((4608, 384), F32),
            pltpu.VMEM((384, 3072), BF),
            pltpu.VMEM((384, 1536), BF),
            pltpu.VMEM((384, 1536), BF),
            pltpu.VMEM((384, 1536), BF),
            pltpu.VMEM((4, 384, 768), BF),
            pltpu.VMEM((4, 16, 48, 768), BF),
            pltpu.VMEM((3072, 384), BF),
            pltpu.VMEM((96, 192), BF),
            dma((9,)),
            dma((6, 25)),
            dma((6, 25)),
            dma((6, 7)),
            dma((6, 7)),
            dma,
            dma,
            dma((4, 7)),
            dma((4, 7)),
            dma((4, 8)),
            dma((4, 8)),
        ],
        compiler_params=pltpu.CompilerParams(
            collective_id=0, has_side_effects=True, vmem_limit_bytes=62 * 2**20
        ),
        name="video_block",
    )(
        spatial_query.reshape(384, 1536),
        spatial_key.reshape(384, 1536),
        spatial_value.reshape(384, 1536),
        tokens.reshape(384, 3072),
        out_weight,
        qkv_weight.T,
        modulation.reshape(72, 128),
        query_gain.reshape(1, 128),
        key_gain.reshape(1, 128),
    )
    out = pl.pallas_call(
        untangle,
        out_shape=jax.ShapeDtypeStruct((384, 1536), BF),
        grid=(3,),
        in_specs=[pl.BlockSpec(memory_space=pltpu.VMEM)],
        out_specs=pl.BlockSpec((128, 1536), lambda i: (i, 0)),
        name="frame_major",
    )(turned)
    return out.reshape(1, 16, 24, 1536)


def solution(mesh):
    placed = (
        P("dp", "seq", None, None),
        P("dp", "seq", None, None),
        P("dp", "seq", None, None),
        P("dp", "seq", None, None),
        P("dp", "seq"),
        P("dp", "seq"),
        P("dp", None, None),
        P(),
        P(),
    )
    return jax.shard_map(
        local, mesh=mesh, in_specs=placed, out_specs=P("dp", None, "seq", None), check_vma=False
    )
```

```python
import functools

import jax
import jax.numpy as jnp
from jax import lax
from jax.experimental import pallas as pl
from jax.experimental.pallas import tpu as pltpu
from jax.sharding import PartitionSpec as P

MESH = pl.DeviceIdType.MESH
BF = jnp.bfloat16
F32 = jnp.float32

W_PIECES = (("yzx", 0, 128, 64), ("zxy", 128, 96, 48), ("xyz", 224, 64, 32))
O_PIECES = (("yzx", 0, 32, 16), ("zxy", 32, 32, 16), ("xyz", 64, 32, 16))


def dot(a, b):
    return jnp.dot(a, b, preferred_element_type=F32)


def kernel(
    q_hbm, k_hbm, v_hbm, tok_hbm, ow_hbm, wt_hbm, mod_hbm, qg_hbm, kg_hbm, ot,
    ow, mods, mod, qg, kg, wbuf, obuf, acc, tok, qs, ks, vs, mix, moved, xt, oin,
    load_sem, ring_s, ring_r, near_s, near_r, oin_s, oin_r, a2a_s, a2a_r, fwd_s, fwd_r,
):
    dp = lax.axis_index("dp")
    seq = lax.axis_index("seq")
    x, z, c = dp // 2, seq // 4, seq % 2
    yl = (seq // 2) % 2
    y = (dp % 2) * 2 + yl
    me = {"x": x, "y": y, "z": z}
    chip = z * 2 + yl

    def device(at, core):
        return (at["x"] * 2 + at["y"] // 2, at["z"] * 4 + (at["y"] % 2) * 2 + core)

    def step(axis, by):
        return {**me, axis: lax.rem(me[axis] + by, 4)}

    def other_chip(t):
        return (dp, t * 2 + c)

    near = device(me, 1 - c)

    parts = (
        (ow_hbm, ow), (wt_hbm, wbuf.at[x, z, y, c]), (q_hbm, qs), (k_hbm, ks), (v_hbm, vs), (tok_hbm, tok),
        (mod_hbm, mods), (qg_hbm, qg), (kg_hbm, kg),
    )
    loads = [pltpu.make_async_copy(src, dst, load_sem.at[i]) for i, (src, dst) in enumerate(parts)]
    for copy in loads:
        copy.start()

    barrier = pltpu.get_barrier_semaphore()
    partners = [device(step(a, by), c) for a in "xyz" for by in (1, 2, 3)] + [near]
    flip = z * 2 + (1 - yl)
    partners += [other_chip(lax.rem(flip + 2 * k, 8)) for k in (1, 2, 3)]
    for partner in partners:
        pl.semaphore_signal(barrier, inc=1, device_id=partner, device_id_type=MESH)
    pl.semaphore_wait(barrier, len(partners))
    loads[0].wait()
    loads[1].wait()

    pending = []

    def remote(src, dst, send, recv, to):
        return pltpu.make_async_remote_copy(
            src_ref=src, dst_ref=dst, send_sem=send, recv_sem=recv, device_id=to, device_id_type=MESH
        )

    def start(src, dst, send, recv, to):
        copy = remote(src, dst, send, recv, to)
        copy.start()
        pending.append(copy)

    def shift(axis, part):
        if axis == "y":
            return (0, 1 + 2 * yl, 3 - 2 * yl, 2)[part]
        return (0, 3, 1, 2)[part]

    def to(axis, way):
        by = (1 + 2 * yl, 3 - 2 * yl)[way] if axis == "y" else (1, 3)[way]
        return device(step(axis, by), c)

    class Piece:
        def __init__(self, buf, spec, base):
            self.buf = buf
            self.order, self.r0, self.n, self.half = spec
            self.base = base

        def slot(self, phase, part, rows="W", group=None, core=None):
            at = dict(me)
            for axis in self.order[:phase]:
                at[axis] = slice(None)
            axis = self.order[phase]
            at[axis] = lax.rem(me[axis] + shift(axis, part), 4)
            if group is not None:
                second = self.order[1]
                at[second] = lax.rem(me[second] + shift(second, group), 4)
            r0, n = {
                "A": (self.r0, self.half),
                "B": (self.r0 + self.half, self.n - self.half),
                "W": (self.r0, self.n),
            }[rows]
            return self.buf.at[at["x"], at["z"], at["y"], c if core is None else core, pl.ds(r0, n), :]

        def sem(self, i):
            return ring_s.at[self.base, i], ring_r.at[self.base, i]

        def send(self, ref, i, target):
            start(ref, ref, *self.sem(i), target)

        def wait(self, ref, i):
            remote(ref, ref, *self.sem(i), near).wait_recv()

        def first(self):
            axis = self.order[0]
            ref = self.slot(0, 0)
            self.send(ref, 0, to(axis, 0))
            self.send(ref, 1, to(axis, 1))
            self.send(ref, 2, device(step(axis, 2), c))

        def first_done(self):
            for part in (1, 2, 3):
                self.wait(self.slot(0, part), part - 1)

        def second(self, k):
            axis = self.order[1]
            for way in range(2):
                    self.send(self.slot(1, 0, "AB"[(way + k) % 2]), 3 + way * 3 + k, to(axis, way))

        def second_on(self):
            axis = self.order[1]
            for way in range(2):
                came = 1 - way if axis == "y" else way
                ref = self.slot(1, 1 + came, "AB"[came])
                self.wait(ref, 3 + came * 3)
                self.send(ref, 3 + way * 3 + 2, to(axis, way))

        def second_sides(self):
            for way in range(2):
                self.wait(self.slot(1, 1 + way, "BA"[way]), 3 + way * 3 + 1)

        def second_far(self):
            axis = self.order[1]
            for way in range(2):
                came = 1 - way if axis == "y" else way
                self.wait(self.slot(1, 3, "AB"[came]), 3 + way * 3 + 2)

        def third(self, group):
            axis = self.order[2]
            for way in range(2):
                self.send(self.slot(2, 0, group=group), 9 + way * 4 + group, to(axis, way))

        def relays(self, way):
            if self.order[2] == "y":
                return ((), (0, 1, 2, 3))[way]
            return ((0, 1), (2, 3))[way]

        def third_on(self, group):
            axis = self.order[2]
            for way in range(2):
                came = 1 - way if axis == "y" else way
                ref = self.slot(2, 1 + came, group=group)
                self.wait(ref, 9 + came * 4 + group)
                if group in self.relays(way):
                    self.send(ref, 17 + way * 4 + group, to(axis, way))

        def third_far(self, group):
            way = 0 if group in self.relays(0) else 1
            self.wait(self.slot(2, 3, group=group), 17 + way * 4 + group)

        def across(self, part, group=None):
            i = part if group is None else 3 + group
            ref = self.slot(2, part, group=group)
            start(ref, ref, near_s.at[self.base, i], near_r.at[self.base, i], near)

        def crossed(self, part, group=None):
            i = part if group is None else 3 + group
            ref = self.slot(2, part, group=group, core=1 - c)
            remote(ref, ref, near_s.at[self.base, i], near_r.at[self.base, i], near).wait_recv()

    ws = [Piece(wbuf, spec, i) for i, spec in enumerate(W_PIECES)]
    os = [Piece(obuf, spec, 3 + i) for i, spec in enumerate(O_PIECES)]

    def each(pieces, name, *args):
        for piece in pieces:
            getattr(piece, name)(*args)

    half = ow.at[pl.ds(pl.multiple_of(96 * (1 - c), 16), 96), :]
    start(half, oin, oin_s, oin_r, near)
    each(ws, "first")
    row = lax.broadcasted_iota(jnp.int32, (192, 384), 0)
    col = lax.broadcasted_iota(jnp.int32, (192, 384), 1)
    mine = ow[pl.ds(pl.multiple_of(96 * c, 16), 96), :]
    block = dot(mine, (col - row == 192 * c).astype(F32).astype(BF))
    remote(oin, oin, oin_s, oin_r, near).wait_recv()
    block += dot(oin[...], (col - row == 192 * (1 - c)).astype(F32).astype(BF))
    obuf[x, z, y, c] = block.astype(BF)
    each(os, "first")

    for copy in loads[2:5]:
        copy.wait()

    def heads(first, count):
        def body(h, _):
            cols = pl.ds(pl.multiple_of(h * 128, 128), 128)
            s = lax.dot_general(
                qs[:, cols], ks[:, cols], (((1,), (1,)), ((), ())), preferred_element_type=F32
            )
            s = s * (128**-0.5)
            e = jnp.exp(s - jnp.max(s, axis=1, keepdims=True))
            total = jnp.sum(e, axis=1, keepdims=True)
            o = dot(e.astype(BF), vs[:, cols])
            qs[:, cols] = (o / total).astype(BF)
            return 0

        lax.fori_loop(first, first + count, body, 0)

    heads(0, 2)
    each(os, "first_done")
    each(os, "second", 0)
    each(os, "second", 1)
    each(os, "third", 0)
    each(ws, "first_done")
    heads(2, 2)
    each(os, "second_on")
    heads(4, 3)
    each(os, "second_sides")
    each(os, "third", 1)
    each(os, "third", 2)
    heads(7, 2)
    each(os, "second_far")
    each(os, "third", 3)
    each(os, "across", 0)
    each(ws, "second", 0)
    each(ws, "second", 1)
    heads(9, 3)
    each(os, "third_on", 0)
    each(ws, "third", 0)
    each(os, "third_on", 1)
    each(os, "third_on", 2)
    each(os, "third_on", 3)
    each(os, "across", 1)
    each(os, "across", 2)
    each(ws, "second_on")
    for group in range(4):
        each(os, "third_far", group)
        each(os, "across", 3, group)
    each(ws, "second_sides")
    each(ws, "third", 1)
    each(ws, "third", 2)
    for part in range(3):
        each(os, "crossed", part)
    for group in range(4):
        each(os, "crossed", 3, group)
    loads[5].wait()
    loads[6].wait()
    for i in range(72):
        mod[i // 24 : i // 24 + 1, i % 24 * 128 : (i % 24 + 1) * 128] = mods[i : i + 1, :]

    def project(zz, _):
        rhs = jnp.concatenate(
            [
                jnp.concatenate(
                    [obuf[xx, zz, yh * 2 + l, cc] for xx in range(4) for yh in range(2) for cc in range(2)],
                    axis=0,
                )
                for l in range(2)
            ],
            axis=1,
        )
        cols = pl.ds(pl.multiple_of(zz * 768, 768), 768)
        proj = dot(qs[...], rhs)
        mix[:, cols] = (tok[:, cols].astype(F32) + mod[0:1, cols] * proj).astype(BF)
        return 0

    lax.fori_loop(0, 4, project, 0)
    each(ws, "second_far")
    each(ws, "third", 3)
    each(ws, "across", 0)
    each(ws, "third_on", 0)

    def normed(t):
        rows = pl.ds(pl.multiple_of(t * 48, 16), 48)
        wide = mix[rows, :].astype(F32)
        mean = jnp.mean(wide, axis=1, keepdims=True)
        dev = wide - mean
        var = jnp.mean(dev * dev, axis=1, keepdims=True)
        return rows, (dev * lax.rsqrt(var + 1e-06) * (1.0 + mod[2:3, :]) + mod[1:2, :]).astype(BF)

    def norm_and_send(i, _):
        t = lax.rem(chip + 1 + i, 8)
        rows, value = normed(t)
        mix[rows, :] = value
        remote(mix.at[rows, :], moved.at[seq], a2a_s.at[i], a2a_r.at[i], other_chip(t)).start()
        return 0

    lax.fori_loop(0, 7, norm_and_send, 0)
    each(ws, "third_on", 1)
    each(ws, "third_on", 2)
    moved[seq] = normed(chip)[1]

    def to_near_rows(i):
        t = lax.rem(chip + 7 - i, 8)
        ref = moved.at[t * 2 + c, pl.ds(pl.multiple_of(16 * (1 - c), 16), 32), :]
        return remote(ref, ref, fwd_s.at[i], fwd_r.at[i], near)

    to_near_rows(7).start()
    each(ws, "third_on", 3)
    each(ws, "across", 1)
    each(ws, "across", 2)

    def pass_on(i, _):
        t = lax.rem(chip + 7 - i, 8)
        ref = moved.at[t * 2 + c]
        remote(ref, ref, a2a_s.at[i], a2a_r.at[i], near).wait_recv()
        to_near_rows(i).start()
        return 0

    lax.fori_loop(0, 7, pass_on, 0)

    def arrive(i, _):
        t = lax.rem(chip + 7 - i, 8)
        ref = moved.at[t * 2 + 1 - c, pl.ds(pl.multiple_of(16 * c, 16), 32), :]
        remote(ref, ref, fwd_s.at[i], fwd_r.at[i], near).wait_recv()
        return 0

    lax.fori_loop(0, 8, arrive, 0)

    m = lax.broadcasted_iota(jnp.int32, (384, 512), 0)
    r = lax.broadcasted_iota(jnp.int32, (384, 512), 1)
    pick = (r == (m & 15) * 32 + (m >> 4) + 8 * c).astype(F32).astype(BF)

    def turn(i, _):
        cols = pl.ds(pl.multiple_of(i * 384, 384), 384)
        rows = moved[:, pl.ds(pl.multiple_of(16 * c, 16), 32), cols].reshape(512, 384)
        xt[cols, :] = dot(pick, rows).astype(BF).T
        return 0

    lax.fori_loop(0, 8, turn, 0)

    def put(rows, value, first):
        if first:
            acc[rows, :] = value
        else:
            acc[rows, :] += value

    def start_row(zz, l, cc, r0):
        return pl.multiple_of(zz * 1152 + l * 576 + cc * 288 + r0, 16)

    def chunk_x(part, group=None):
        _, r0, n, _ = W_PIECES[0]
        xx = lax.rem(x + shift("x", part), 4)
        rhs_rows = pl.ds(pl.multiple_of(xx * 768, 768), 768)

        def body(zz, _):
            lhs = jnp.concatenate(
                [
                    jnp.concatenate([wbuf[xx, zz, yh * 2 + l, cc, r0 : r0 + n, :] for yh in range(2)], axis=1)
                    for l in range(2)
                    for cc in range(2)
                ],
                axis=0,
            )
            res = dot(lhs, xt[rhs_rows, :])
            for i in range(4):
                put(pl.ds(start_row(zz, i // 2, i % 2, r0), n), res[i * n : (i + 1) * n], part == 0)
            return 0

        if group is None:
            lax.fori_loop(0, 4, body, 0)
        else:
            body(lax.rem(z + shift("z", group), 4), 0)

    def chunk_y(part):
        first = part < 2
        _, r0, n, _ = W_PIECES[1]
        yy = lax.rem(y + shift("y", part), 4)
        hi, lo = yy // 2, yy % 2
        rhs = jnp.concatenate(
            [xt[pl.ds(pl.multiple_of(xx * 768 + hi * 384, 384), 384), :] for xx in range(4)], axis=0
        )

        def body(zp, _):
            lhs = jnp.concatenate(
                [
                    jnp.concatenate([wbuf[xx, zp * 2 + zz, yy, cc, r0 : r0 + n, :] for xx in range(4)], axis=1)
                    for zz in range(2)
                    for cc in range(2)
                ],
                axis=0,
            )
            res = dot(lhs, rhs)
            for i in range(4):
                put(pl.ds(start_row(zp * 2 + i // 2, lo, i % 2, r0), n), res[i * n : (i + 1) * n], first)
            return 0

        lax.fori_loop(0, 2, body, 0)

    def near_x():
        _, r0, n, _ = W_PIECES[0]
        places = [lax.rem(x + shift("x", part), 4) for part in range(3)]
        rhs = jnp.concatenate([xt[pl.ds(pl.multiple_of(xx * 768, 768), 768), :] for xx in places], axis=0)

        def body(i, _):
            zz, l = i // 2, i % 2
            lhs = jnp.concatenate(
                [
                    jnp.concatenate(
                        [wbuf[xx, zz, yh * 2 + l, cc, r0 : r0 + n, :] for xx in places for yh in range(2)], axis=1
                    )
                    for cc in range(2)
                ],
                axis=0,
            )
            res = dot(lhs, rhs)
            for cc in range(2):
                put(pl.ds(start_row(zz, l, cc, r0), n), res[cc * n : (cc + 1) * n], True)
            return 0

        lax.fori_loop(0, 8, body, 0)

    def sides_y():
        _, r0, n, _ = W_PIECES[1]
        places = [lax.rem(y + shift("y", part), 4) for part in (1, 2)]
        rhs = jnp.concatenate(
            [
                xt[pl.ds(pl.multiple_of(xx * 768 + yy // 2 * 384, 384), 384), :]
                for yy in places
                for xx in range(4)
            ],
            axis=0,
        )

        def body(zz, _):
            lhs = jnp.concatenate(
                [
                    jnp.concatenate(
                        [wbuf[xx, zz, yy, cc, r0 : r0 + n, :] for yy in places for xx in range(4)], axis=1
                    )
                    for cc in range(2)
                ],
                axis=0,
            )
            res = dot(lhs, rhs)
            for cc in range(2):
                put(pl.ds(start_row(zz, 1 - yl, cc, r0), n), res[cc * n : (cc + 1) * n], True)
            return 0

        lax.fori_loop(0, 4, body, 0)

    def chunk_z(part):
        _, r0, n, _ = W_PIECES[2]
        zz = lax.rem(z + shift("z", part), 4)
        lhs = jnp.concatenate(
            [
                jnp.concatenate(
                    [wbuf[xx, zz, yh * 2 + l, cc, r0 : r0 + n, :] for xx in range(4) for yh in range(2)], axis=1
                )
                for l in range(2)
                for cc in range(2)
            ],
            axis=0,
        )
        res = dot(lhs, xt[...])
        for i in range(4):
            put(pl.ds(start_row(zz, i // 2, i % 2, r0), n), res[i * n : (i + 1) * n], True)

    for part in range(3):
        each(ws, "crossed", part)
    each(ws, "third_far", 0)
    each(ws, "across", 3, 0)
    near_x()
    each(ws, "third_far", 1)
    each(ws, "across", 3, 1)
    chunk_y(0)
    sides_y()
    each(ws, "third_far", 2)
    each(ws, "across", 3, 2)
    for part in range(3):
        chunk_z(part)
    each(ws, "third_far", 3)
    each(ws, "across", 3, 3)
    for group in range(3):
        each(ws[:1], "crossed", 3, group)
        chunk_x(3, group)
    for group in range(4):
        each(ws[1:], "crossed", 3, group)
    chunk_y(3)
    chunk_z(3)
    each(ws[:1], "crossed", 3, 3)
    chunk_x(3, 3)
    loads[7].wait()
    loads[8].wait()

    def unit(rows, gain):
        wide = acc[rows, :].astype(BF).astype(F32)
        scale = lax.rsqrt(jnp.sum(wide * wide, axis=0, keepdims=True) * (1.0 / 128) + 1e-06)
        return (wide * scale * gain).astype(BF)

    def column(gain):
        return jnp.concatenate([jnp.broadcast_to(gain[...], (128, 128)).T] * 3, axis=1)

    qcol, kcol = column(qg), column(kg)
    ii = lax.broadcasted_iota(jnp.int32, (128, 128), 0)
    jj = lax.broadcasted_iota(jnp.int32, (128, 128), 1)
    same = (ii >> 4) == (jj >> 4)

    def temporal(h):
        rows = pl.multiple_of(h * 128, 128)
        q = unit(pl.ds(rows, 128), qcol)
        k = unit(pl.ds(1536 + rows, 128), kcol)
        v = acc[pl.ds(3072 + rows, 128), :].astype(BF)
        for g in range(3):
            cols = slice(g * 128, (g + 1) * 128)
            s = dot(k[:, cols].T, q[:, cols]) * (128**-0.5)
            s = jnp.where(same, s, -1e30)
            e = jnp.exp(s - jnp.max(s, axis=0, keepdims=True))
            p = (e / jnp.sum(e, axis=0, keepdims=True)).astype(BF)
            ot[pl.ds(rows, 128), cols] = dot(v[:, cols], p).astype(BF)

    def two_heads(i, _):
        temporal(i * 2)
        temporal(i * 2 + 1)
        return 0

    lax.fori_loop(0, 6, two_heads, 0)

    for copy in pending:
        copy.wait_send()

    def sent(i, _):
        t = lax.rem(chip + 1 + i, 8)
        rows = pl.ds(pl.multiple_of(t * 48, 16), 48)
        remote(mix.at[rows, :], moved.at[seq], a2a_s.at[i], a2a_r.at[i], other_chip(t)).wait_send()
        return 0

    lax.fori_loop(0, 7, sent, 0)

    def sent_near(i, _):
        to_near_rows(i).wait_send()
        return 0

    lax.fori_loop(0, 8, sent_near, 0)


def untangle(ot, out):
    a = lax.broadcasted_iota(jnp.int32, (128, 384), 0) + pl.program_id(0) * 128
    b = lax.broadcasted_iota(jnp.int32, (128, 384), 1)
    back = (a == (b & 15) * 24 + (b >> 4)).astype(F32).astype(BF)
    out[...] = lax.dot_general(back, ot[...], (((1,), (1,)), ((), ())), preferred_element_type=F32).astype(BF)


def local(
    tokens, spatial_query, spatial_key, spatial_value, out_weight, qkv_weight, modulation, query_gain, key_gain
):
    hbm = pl.BlockSpec(memory_space=pl.ANY)
    dma = pltpu.SemaphoreType.DMA
    turned = pl.pallas_call(
        kernel,
        out_shape=jax.ShapeDtypeStruct((1536, 384), BF),
        in_specs=[hbm] * 9,
        out_specs=pl.BlockSpec(memory_space=pltpu.VMEM),
        scratch_shapes=[
            pltpu.VMEM((192, 192), BF),
            pltpu.VMEM((72, 128), F32),
            pltpu.VMEM((8, 3072), F32),
            pltpu.VMEM((1, 128), F32),
            pltpu.VMEM((1, 128), F32),
            pltpu.VMEM((4, 4, 4, 2, 288, 384), BF),
            pltpu.VMEM((4, 4, 4, 2, 96, 384), BF),
            pltpu.VMEM((4608, 384), F32),
            pltpu.VMEM((384, 3072), BF),
            pltpu.VMEM((384, 1536), BF),
            pltpu.VMEM((384, 1536), BF),
            pltpu.VMEM((384, 1536), BF),
            pltpu.VMEM((384, 3072), BF),
            pltpu.VMEM((16, 48, 3072), BF),
            pltpu.VMEM((3072, 384), BF),
            pltpu.VMEM((96, 192), BF),
            dma((9,)),
            dma((6, 25)),
            dma((6, 25)),
            dma((6, 7)),
            dma((6, 7)),
            dma,
            dma,
            dma((7,)),
            dma((7,)),
            dma((8,)),
            dma((8,)),
        ],
        compiler_params=pltpu.CompilerParams(
            collective_id=0, has_side_effects=True, vmem_limit_bytes=62 * 2**20
        ),
        name="video_block",
    )(
        spatial_query.reshape(384, 1536),
        spatial_key.reshape(384, 1536),
        spatial_value.reshape(384, 1536),
        tokens.reshape(384, 3072),
        out_weight,
        qkv_weight.T,
        modulation.reshape(72, 128),
        query_gain.reshape(1, 128),
        key_gain.reshape(1, 128),
    )
    out = pl.pallas_call(
        untangle,
        out_shape=jax.ShapeDtypeStruct((384, 1536), BF),
        grid=(3,),
        in_specs=[pl.BlockSpec(memory_space=pltpu.VMEM)],
        out_specs=pl.BlockSpec((128, 1536), lambda i: (i, 0)),
        name="frame_major",
    )(turned)
    return out.reshape(1, 16, 24, 1536)


def solution(mesh):
    placed = (
        P("dp", "seq", None, None),
        P("dp", "seq", None, None),
        P("dp", "seq", None, None),
        P("dp", "seq", None, None),
        P("dp", "seq"),
        P("dp", "seq"),
        P("dp", None, None),
        P(),
        P(),
    )
    return jax.shard_map(
        local, mesh=mesh, in_specs=placed, out_specs=P("dp", None, "seq", None), check_vma=False
    )
```
